32 devices in a mesh: section: 8 (over y, x, core), dp: 4 (over z).
Axes of the slice: x: 2, y: 2, z: 4, core: 2. Of those that a mesh axis runs over, the one named last changes fastest.
Arguments:
- saved_x: bfloat16 [2, 3, 8, 4, 16, 16, 128], P(None, None, 'section', 'dp'), may hold values from -6 to 6
- saved_h: bfloat16 [2, 3, 8, 4, 16, 16, 128], P(None, None, 'section', 'dp'), may hold values from -6 to 6
- kernels: bfloat16 [8, 2, 2, 9, 128, 128], P('section'), as said below
- grad_in: bfloat16 [2, 8, 4, 16, 16, 128], P(None, 'section', 'dp'), may hold values from -6 to 6
- loss_grads: bfloat16 [2, 2, 4, 16, 16, 128], P(None, None, 'dp'), may hold values from -6 to 6
Outputs:
- kernel_grads: float32 [8, 2304, 128], P('section', 'dp')
- edge_grads: bfloat16 [2, 8, 4, 16, 16, 128], P(None, 'section', 'dp')
The draws below stay inside these ranges and needn't reach their ends.
Inputs may be any that keep to these rules, and one draw needn't show every extreme that they name: kernels[d, 1] equals kernels[7 - d, 0]: each position holds replica 1's copy of the mirrored section. Every entry lies within 3 / sqrt(1152) in magnitude.
All inputs are finite; a program needn't handle non-finite values.
Results may differ from the reference program's by a relative error of at most 0.0052.
Values may be sent and summed in bfloat16 or wider, within the bound.
A program may use at most 64 MiB of HBM per device.

```python
import jax
import jax.numpy as jnp
from jax import lax

C = 128
TILE = 16
TICKS = 3
SECTIONS = 8
BATCH = 4


def draw_kernels(key, part):
    base = jnp.clip(jax.random.normal(key, (SECTIONS, 2, 9, C, C), jnp.float32), -3.0, 3.0) * (9 * C) ** (-0.5)
    return jnp.stack([base, base[::-1]], axis=1).astype(jnp.bfloat16)


def shard_levels(rng, shape, cuts, low, top_value):
    level = 1.0
    for axis_at, blocks in cuts:
        steps = jax.random.uniform(jax.random.fold_in(jax.random.fold_in(rng, 6), axis_at), (blocks,), jnp.float32, low / len(cuts), top_value / len(cuts))
        level = level * jnp.repeat(jnp.exp(steps), shape[axis_at] // blocks).reshape((-1,) + (1,) * (len(shape) - 1 - axis_at))
    return level


def gaussian(stream_key, shape, width, bound, shards=(), dtype=jnp.bfloat16):
    result = jax.random.normal(stream_key, shape, jnp.float32) * width
    if len(shards) > 0:
        result = shard_levels(stream_key, shape, shards, -0.22, 0.18) * result
    return jnp.clip(result, min=-bound, max=bound).astype(dtype)


def setup_inputs(seed: int = 0) -> dict:
    key_list = jax.random.split(jax.random.key(seed), 6)
    saved_x = gaussian(key_list[0], (2, TICKS, SECTIONS, BATCH, TILE, TILE, C), 1.0, 6.0, ((2, 8), (3, 4)))
    saved_h = gaussian(key_list[1], (2, TICKS, SECTIONS, BATCH, TILE, TILE, C), 1.0, 6.0, ((2, 8), (3, 4)))
    kernels = draw_kernels(jax.random.fold_in(key_list[5], 71), 0)
    grad_in = gaussian(key_list[3], (2, SECTIONS, BATCH, TILE, TILE, C), 1.0, 6.0, ((1, 8), (2, 4)))
    loss_grads = gaussian(key_list[4], (2, TICKS - 1, BATCH, TILE, TILE, C), 1.0, 6.0, ((2, 4),))
    return dict(saved_x=saved_x, saved_h=saved_h, kernels=kernels, grad_in=grad_in, loss_grads=loss_grads)


highest = lax.Precision.HIGHEST


def tap_views(feature, sign):
    extent = feature.shape[1]
    padded = jnp.pad(feature, ((0, 0), (1, 1), (1, 1), (0, 0)))
    pieces = []
    for row_shift in (-1, 0, 1):
        for col_shift in (-1, 0, 1):
            row_start = 1 + sign * row_shift
            col_start = 1 + sign * col_shift
            pieces.append(padded[:, row_start:row_start + extent, col_start:col_start + extent, :])
    return jnp.stack(pieces, axis=3)


def block_back(grad_out, inputs, hidden, w_first, w_second):
    act_h = jnp.maximum(hidden, 0)
    act_x = jnp.maximum(inputs, 0)
    grad_z = jnp.einsum('byxkd,kcd->byxc', tap_views(grad_out, -1).astype(jnp.float32), w_second.astype(jnp.float32), precision=highest)
    g_second = jnp.einsum('byxkc,byxd->kcd', tap_views(act_h, 1).astype(jnp.float32), grad_out.astype(jnp.float32), precision=highest)
    grad_h = jnp.where(hidden > 0, grad_z, 0.0).astype(jnp.bfloat16)
    grad_u = jnp.einsum('byxkd,kcd->byxc', tap_views(grad_h, -1).astype(jnp.float32), w_first.astype(jnp.float32), precision=highest)
    g_first = jnp.einsum('byxkc,byxd->kcd', tap_views(act_x, 1).astype(jnp.float32), grad_h.astype(jnp.float32), precision=highest)
    grad_x = (grad_out.astype(jnp.float32) + jnp.where(inputs > 0, grad_u, 0.0)).astype(jnp.bfloat16)
    return grad_x, jnp.stack([g_first, g_second])


def section_back(pieces):
    return block_back(pieces[0], pieces[1], pieces[2], pieces[3], pieces[4])


def reference(saved_x, saved_h, kernels, grad_in, loss_grads):
    ticks_total = saved_x.shape[1]
    totals = [None, None]
    outgoing = None
    for tick_index in range(ticks_total):
        if tick_index == 0:
            incoming = [grad_in[0], grad_in[1]]
        else:
            incoming = [jnp.concatenate([outgoing[0][1:], loss_grads[0, tick_index - 1][None]], axis=0),
                        jnp.concatenate([loss_grads[1, tick_index - 1][None], outgoing[1][:-1]], axis=0)]
        new_out = []
        for replica in range(2):
            grad_x, grads = lax.map(section_back, (incoming[replica], saved_x[replica, tick_index], saved_h[replica, tick_index], kernels[:, replica, 0], kernels[:, replica, 1]))
            totals[replica] = grads if tick_index == 0 else totals[replica] + grads
            new_out.append(grad_x)
        outgoing = new_out
    summed = totals[0] + totals[1][::-1]
    extent = saved_x.shape[4]
    kernel_grads = (summed / float(extent * extent)).reshape(summed.shape[0], -1, summed.shape[-1])
    return kernel_grads, jnp.stack(outgoing)
```

```python
import functools

import jax
import jax.numpy as jnp
from jax import lax
from jax.experimental import pallas as pl
from jax.experimental.pallas import tpu as pltpu
from jax.sharding import PartitionSpec as P

MESH = pl.DeviceIdType.MESH
F32 = jnp.float32
BF16 = jnp.bfloat16


def dims(cfg):
    return cfg["S"], cfg["N"], cfg["T"], cfg["E"], cfg["C"]


def relay(cfg, x_hbm, h_hbm, w_hbm, g_hbm, l_hbm, kg_ref, edge_hbm,
          xs, hs, gs, ob, wc, vb, acc, rr, rl, sr, sl,
          in_sem, w_sem, l_sem, ms, mr, ts, tr, es, er, lsem, rs_s, rs_r, ls_s, ls_r):
    S, N, T, E, C = dims(cfg)
    M = E * E
    R = 18 * C // N
    me_s = lax.axis_index("section")
    me_p = lax.axis_index("dp")
    mirror = S - 1 - me_s
    first = me_s == 0
    last = me_s == S - 1

    local = {}
    local["g"] = pltpu.make_async_copy(g_hbm.at[0], gs.at[0, 0], in_sem.at[0])
    for t in range(T):
        local["h", t] = pltpu.make_async_copy(h_hbm.at[0, t], hs.at[t, 0], in_sem.at[1 + 2 * t])
        local["x", t] = pltpu.make_async_copy(x_hbm.at[0, t], xs.at[t, 0], in_sem.at[2 + 2 * t])
    weights = []
    for pair in range(2):
        weights.append([
            pltpu.make_async_copy(
                w_hbm.at[0, pair, k], wc.at[pair, :, pl.ds(k * C, C)], w_sem.at[pair, k])
            for k in range(9)
        ])
    losses = {
        (t, r): pltpu.make_async_copy(l_hbm.at[r, t - 1], gs.at[t, r], l_sem.at[t - 1, r])
        for t in range(1, T) for r in range(2)
    }
    local["g"].start()
    for c in weights[1]:
        c.start()
    local["h", 0].start()
    for c in weights[0]:
        c.start()
    local["x", 0].start()
    for t in range(1, T):
        local["h", t].start()
        local["x", t].start()

    @pl.when(last)
    def _():
        for c in losses.values():
            c.start()

    barrier = pltpu.get_barrier_semaphore()
    pl.semaphore_signal(barrier, inc=1, device_id=(mirror, me_p), device_id_type=MESH)

    @pl.when(me_s > 0)
    def _():
        pl.semaphore_signal(barrier, inc=1, device_id=(me_s - 1, me_p), device_id_type=MESH)

    @pl.when(me_s < S - 1)
    def _():
        pl.semaphore_signal(barrier, inc=1, device_id=(me_s + 1, me_p), device_id_type=MESH)

    @pl.when(me_p > 0)
    def _():
        pl.semaphore_signal(barrier, inc=1, device_id=(me_s, me_p - 1), device_id_type=MESH)

    @pl.when(me_p < N - 1)
    def _():
        pl.semaphore_signal(barrier, inc=1, device_id=(me_s, me_p + 1), device_id_type=MESH)

    greeted = (1 + (me_s > 0).astype(jnp.int32) + (me_s < S - 1).astype(jnp.int32)
               + (me_p > 0).astype(jnp.int32) + (me_p < N - 1).astype(jnp.int32))
    pl.semaphore_wait(barrier, greeted)

    def to_mirror(src, dst, i):
        return pltpu.make_async_remote_copy(
            src_ref=src, dst_ref=dst, send_sem=ms.at[i], recv_sem=mr.at[i],
            device_id=(mirror, me_p), device_id_type=MESH)

    moved = {"g": to_mirror(g_hbm.at[1], gs.at[0, 1], 0)}
    for t in range(T):
        moved["h", t] = to_mirror(h_hbm.at[1, t], hs.at[t, 1], 1 + 2 * t)
        moved["x", t] = to_mirror(x_hbm.at[1, t], xs.at[t, 1], 2 + 2 * t)
    for c in moved.values():
        c.start()

    steps = {
        (t, r): pltpu.make_async_remote_copy(
            src_ref=ob.at[t, r], dst_ref=gs.at[t + 1, r], send_sem=ts.at[t, r],
            recv_sem=tr.at[t, r], device_id=(me_s - 1, me_p), device_id_type=MESH)
        for t in range(T - 1) for r in range(2)
    }
    edge_home = pltpu.make_async_copy(ob.at[T - 1, 0], edge_hbm.at[0], lsem.at[0])
    edge_away = pltpu.make_async_remote_copy(
        src_ref=ob.at[T - 1, 1], dst_ref=edge_hbm.at[1], send_sem=es.at[0], recv_sem=er.at[0],
        device_id=(mirror, me_p), device_id_type=MESH)

    def right(q):
        return pltpu.make_async_remote_copy(
            src_ref=sr.at[q], dst_ref=rr.at[q], send_sem=rs_s.at[q], recv_sem=rs_r.at[q],
            device_id=(me_s, me_p + 1), device_id_type=MESH)

    def left(q):
        return pltpu.make_async_remote_copy(
            src_ref=sl.at[q], dst_ref=rl.at[q], send_sem=ls_s.at[q], recv_sem=ls_r.at[q],
            device_id=(me_s, me_p - 1), device_id_type=MESH)

    column = lax.broadcasted_iota(jnp.int32, (M, C), 0) % E
    low = column == 0
    high = column == E - 1
    for i in range(4):
        vb[i, 0:E, :] = jnp.zeros((E, 3 * C), BF16)
        vb[i, E + M:2 * E + M, :] = jnp.zeros((E, 3 * C), BF16)

    def spread(i, value):
        back = jnp.where(high, 0.0, pltpu.roll(value, M - 1, axis=0))
        ahead = jnp.where(low, 0.0, pltpu.roll(value, 1, axis=0))
        vb[i, E:E + M, 0:C] = back.astype(BF16)
        vb[i, E:E + M, C:2 * C] = value.astype(BF16)
        vb[i, E:E + M, 2 * C:3 * C] = ahead.astype(BF16)

    def rows(i, j):
        start = E - E * (j - 1)
        return vb[i, start:start + M, :]

    def conv(i, pair):
        total = None
        for j in range(3):
            part = lax.dot_general(
                rows(i, j), wc[pair, :, 3 * C * j:3 * C * (j + 1)],
                (((1,), (1,)), ((), ())), preferred_element_type=F32)
            total = part if total is None else total + part
        return total

    def weight_grad(i, pair, act, fresh):
        turned = jnp.maximum(act, 0).T
        for j in range(3):
            part = jnp.dot(turned, rows(i, j), preferred_element_type=F32)
            for d in range(3):
                at = (pair * 9 + 3 * j + d) * C
                piece = part[:, d * C:(d + 1) * C]
                if fresh:
                    acc[at:at + C, :] = piece
                else:
                    acc[at:at + C, :] += piece

    def own(q):
        return acc[q * R:(q + 1) * R, :]

    for t in range(T):
        for r in range(2):
            final = t == T - 1
            source = local if r == 0 else moved

            def arrived(name):
                if r == 0:
                    local[name].wait()
                else:
                    moved[name].wait_recv()

            if t == 0:
                arrived("g")
            else:
                @pl.when(last)
                def _():
                    losses[t, r].wait()

                @pl.when(jnp.logical_not(last))
                def _():
                    steps[t - 1, r].wait_recv()
            ga, gb = 2 * r, 2 * r + 1
            grad = gs[t, r].astype(F32)
            spread(ga, grad)
            if t == 0 and r == 0:
                for c in weights[1]:
                    c.wait()
            arrived(("h", t))
            hidden = hs[t, r]
            fresh = t == 0 and r == 0
            if final:
                weight_grad(ga, 1, hidden, fresh)
                if r == 1:
                    @pl.when(me_p == 0)
                    def _():
                        for q in range(N - 1, N // 2 - 1, -1):
                            if q > 0:
                                sr[q] = own(q).astype(BF16)
                                right(q).start()
            grad_h = jnp.where(hidden.astype(F32) > 0, conv(ga, 1), 0.0)
            spread(gb, grad_h)
            if t == 0 and r == 0:
                for c in weights[0]:
                    c.wait()
            arrived(("x", t))
            inputs = xs[t, r]
            if final:
                weight_grad(gb, 0, inputs, fresh)
                if r == 1:
                    @pl.when(me_p == 0)
                    def _():
                        for q in range(N // 2 - 1, 0, -1):
                            sr[q] = own(q).astype(BF16)
                            right(q).start()

                    @pl.when(me_p == N - 1)
                    def _():
                        for q in range(N - 1):
                            sl[q] = own(q).astype(BF16)
                            left(q).start()
            grad_u = conv(gb, 0)
            ob[t, r] = (grad + jnp.where(inputs.astype(F32) > 0, grad_u, 0.0)).astype(BF16)
            if final:
                if r == 0:
                    edge_home.start()
                else:
                    edge_away.start()
            else:
                @pl.when(me_s > 0)
                def _():
                    steps[t, r].start()

                weight_grad(ga, 1, hidden, fresh)
                weight_grad(gb, 0, inputs, fresh)

    inner = jnp.logical_and(me_p > 0, me_p < N - 1)
    for i in range(N - 1):
        up, down = N - 1 - i, i

        @pl.when(jnp.logical_and(inner, up > me_p))
        def _():
            right(up).wait_recv()
            sr[up] = (own(up) + rr[up].astype(F32)).astype(BF16)
            right(up).start()

        @pl.when(jnp.logical_and(inner, down < me_p))
        def _():
            left(down).wait_recv()
            sl[down] = (own(down) + rl[down].astype(F32)).astype(BF16)
            left(down).start()

    scale = 1.0 / float(E * E)
    for q in range(N):
        @pl.when(me_p == q)
        def _():
            total = own(q)
            if q > 0:
                right(q).wait_recv()
                total = total + rr[q].astype(F32)
            if q < N - 1:
                left(q).wait_recv()
                total = total + rl[q].astype(F32)
            kg_ref[...] = total * scale

    edge_home.wait()
    edge_away.wait()
    for c in moved.values():
        c.wait_send()

    @pl.when(me_s > 0)
    def _():
        for c in steps.values():
            c.wait_send()

    for q in range(N):
        @pl.when(q > me_p)
        def _():
            right(q).wait_send()

        @pl.when(q < me_p)
        def _():
            left(q).wait_send()


def on_device(saved_x, saved_h, kernels, grad_in, loss_grads):
    S, N = lax.axis_size("section"), lax.axis_size("dp")
    T, E, C = saved_x.shape[1], saved_x.shape[4], saved_x.shape[6]
    M = E * E * saved_x.shape[3]
    R = 18 * C // N
    cfg = dict(S=S, N=N, T=T, E=E, C=C)
    DMA = pltpu.SemaphoreType.DMA
    kg, edge = pl.pallas_call(
        functools.partial(relay, cfg),
        out_shape=(jax.ShapeDtypeStruct((R, C), F32), jax.ShapeDtypeStruct((2, M, C), BF16)),
        in_specs=[pl.BlockSpec(memory_space=pl.ANY)] * 5,
        out_specs=(pl.BlockSpec(memory_space=pltpu.VMEM), pl.BlockSpec(memory_space=pl.ANY)),
        scratch_shapes=[
            pltpu.VMEM((T, 2, M, C), BF16),
            pltpu.VMEM((T, 2, M, C), BF16),
            pltpu.VMEM((T, 2, M, C), BF16),
            pltpu.VMEM((T, 2, M, C), BF16),
            pltpu.VMEM((2, C, 9 * C), BF16),
            pltpu.VMEM((4, M + 2 * E, 3 * C), BF16),
            pltpu.VMEM((18 * C, C), F32),
            pltpu.VMEM((N, R, C), BF16),
            pltpu.VMEM((N, R, C), BF16),
            pltpu.VMEM((N, R, C), BF16),
            pltpu.VMEM((N, R, C), BF16),
            DMA((2 * T + 1,)),
            DMA((2, 9)),
            DMA((T, 2)),
            DMA((2 * T + 1,)),
            DMA((2 * T + 1,)),
            DMA((T, 2)),
            DMA((T, 2)),
            DMA((1,)),
            DMA((1,)),
            DMA((1,)),
            DMA((N,)),
            DMA((N,)),
            DMA((N,)),
            DMA((N,)),
        ],
        compiler_params=pltpu.CompilerParams(
            collective_id=0, has_side_effects=True, vmem_limit_bytes=40 * 1024 * 1024),
        cost_estimate=pl.CostEstimate(
            flops=48 * T * M * 9 * C * C // 6, bytes_accessed=3_000_000, transcendentals=0),
        name="relay",
    )(
        saved_x.reshape(2, T, M, C),
        saved_h.reshape(2, T, M, C),
        kernels.reshape(2, 2, 9, C, C),
        grad_in.reshape(2, M, C),
        loss_grads.reshape(2, T - 1, M, C),
    )
    return kg[None], edge.reshape(2, 1, 1, E, E, C)


def solution(mesh):
    return jax.shard_map(
        on_device,
        mesh=mesh,
        in_specs=(
            P(None, None, "section", "dp", None, None, None),
            P(None, None, "section", "dp", None, None, None),
            P("section", None, None, None, None, None),
            P(None, "section", "dp", None, None, None),
            P(None, None, "dp", None, None, None),
        ),
        out_specs=(P("section", "dp", None), P(None, "section", "dp", None, None, None)),
        check_vma=False,
    )
```

```python
import functools

import jax
import jax.numpy as jnp
from jax import lax
from jax.experimental import pallas as pl
from jax.experimental.pallas import tpu as pltpu
from jax.sharding import PartitionSpec as P

MESH = pl.DeviceIdType.MESH
F32 = jnp.float32
BF16 = jnp.bfloat16


def dims(cfg):
    return cfg["S"], cfg["N"], cfg["T"], cfg["E"], cfg["C"]


def relay(cfg, x_hbm, h_hbm, w_hbm, g_hbm, l_hbm, kg_ref, edge_hbm,
          xs, hs, gs, ob, wc, vb, acc, rr, sr,
          in_sem, w_sem, l_sem, ms, mr, ts, tr, es, er, lsem, rs_s, rs_r):
    S, N, T, E, C = dims(cfg)
    M = E * E
    R = 18 * C // N
    me_s = lax.axis_index("section")
    me_p = lax.axis_index("dp")
    mirror = S - 1 - me_s
    first = me_s == 0
    last = me_s == S - 1

    local = {}
    local["g"] = pltpu.make_async_copy(g_hbm.at[0], gs.at[0, 0], in_sem.at[0])
    for t in range(T):
        local["h", t] = pltpu.make_async_copy(h_hbm.at[0, t], hs.at[t, 0], in_sem.at[1 + 2 * t])
        local["x", t] = pltpu.make_async_copy(x_hbm.at[0, t], xs.at[t, 0], in_sem.at[2 + 2 * t])
    weights = []
    for pair in range(2):
        weights.append([
            pltpu.make_async_copy(
                w_hbm.at[0, pair, k], wc.at[pair, :, pl.ds(k * C, C)], w_sem.at[pair, k])
            for k in range(9)
        ])
    losses = {
        (t, r): pltpu.make_async_copy(l_hbm.at[r, t - 1], gs.at[t, r], l_sem.at[t - 1, r])
        for t in range(1, T) for r in range(2)
    }
    local["g"].start()
    for c in weights[1]:
        c.start()
    local["h", 0].start()
    for c in weights[0]:
        c.start()
    local["x", 0].start()
    for t in range(1, T):
        local["h", t].start()
        local["x", t].start()

    @pl.when(last)
    def _():
        for c in losses.values():
            c.start()

    barrier = pltpu.get_barrier_semaphore()
    pl.semaphore_signal(barrier, inc=1, device_id=(mirror, me_p), device_id_type=MESH)

    @pl.when(me_s > 0)
    def _():
        pl.semaphore_signal(barrier, inc=1, device_id=(me_s - 1, me_p), device_id_type=MESH)

    @pl.when(me_s < S - 1)
    def _():
        pl.semaphore_signal(barrier, inc=1, device_id=(me_s + 1, me_p), device_id_type=MESH)

    for q in range(N):
        @pl.when(me_p != q)
        def _():
            pl.semaphore_signal(barrier, inc=1, device_id=(me_s, q), device_id_type=MESH)

    greeted = N + (me_s > 0).astype(jnp.int32) + (me_s < S - 1).astype(jnp.int32)
    pl.semaphore_wait(barrier, greeted)

    def to_mirror(src, dst, i):
        return pltpu.make_async_remote_copy(
            src_ref=src, dst_ref=dst, send_sem=ms.at[i], recv_sem=mr.at[i],
            device_id=(mirror, me_p), device_id_type=MESH)

    moved = {"g": to_mirror(g_hbm.at[1], gs.at[0, 1], 0)}
    for t in range(T):
        moved["h", t] = to_mirror(h_hbm.at[1, t], hs.at[t, 1], 1 + 2 * t)
        moved["x", t] = to_mirror(x_hbm.at[1, t], xs.at[t, 1], 2 + 2 * t)
    groups = [["g", ("h", 0), ("x", 0)]] + [[("h", t), ("x", t)] for t in range(1, T)]

    def send_group(t):
        if t < T:
            for name in groups[t]:
                moved[name].start()

    send_group(0)
    send_group(1)

    steps = {
        (t, r): pltpu.make_async_remote_copy(
            src_ref=ob.at[t, r], dst_ref=gs.at[t + 1, r], send_sem=ts.at[t, r],
            recv_sem=tr.at[t, r], device_id=(me_s - 1, me_p), device_id_type=MESH)
        for t in range(T - 1) for r in range(2)
    }
    edge_home = pltpu.make_async_copy(ob.at[T - 1, 0], edge_hbm.at[0], lsem.at[0])
    edge_away = pltpu.make_async_remote_copy(
        src_ref=ob.at[T - 1, 1], dst_ref=edge_hbm.at[1], send_sem=es.at[0], recv_sem=er.at[0],
        device_id=(mirror, me_p), device_id_type=MESH)

    def to_owner(q):
        return pltpu.make_async_remote_copy(
            src_ref=sr.at[q], dst_ref=rr.at[me_p], send_sem=rs_s.at[q], recv_sem=rs_r.at[me_p],
            device_id=(me_s, q), device_id_type=MESH)

    def from_shard(p):
        return pltpu.make_async_remote_copy(
            src_ref=sr.at[p], dst_ref=rr.at[p], send_sem=rs_s.at[p], recv_sem=rs_r.at[p],
            device_id=(me_s, p), device_id_type=MESH)

    column = lax.broadcasted_iota(jnp.int32, (M, C), 0) % E
    low = column == 0
    high = column == E - 1
    for i in range(4):
        vb[i, 0:E, :] = jnp.zeros((E, 3 * C), BF16)
        vb[i, E + M:2 * E + M, :] = jnp.zeros((E, 3 * C), BF16)

    def spread(i, value):
        back = jnp.where(high, 0.0, pltpu.roll(value, M - 1, axis=0))
        ahead = jnp.where(low, 0.0, pltpu.roll(value, 1, axis=0))
        vb[i, E:E + M, 0:C] = back.astype(BF16)
        vb[i, E:E + M, C:2 * C] = value.astype(BF16)
        vb[i, E:E + M, 2 * C:3 * C] = ahead.astype(BF16)

    def rows(i, j):
        start = E - E * (j - 1)
        return vb[i, start:start + M, :]

    def conv(i, pair):
        total = None
        for j in range(3):
            part = lax.dot_general(
                rows(i, j), wc[pair, :, 3 * C * j:3 * C * (j + 1)],
                (((1,), (1,)), ((), ())), preferred_element_type=F32)
            total = part if total is None else total + part
        return total

    def weight_grad(i, pair, act, fresh):
        turned = jnp.maximum(act, 0).T
        for j in range(3):
            part = jnp.dot(turned, rows(i, j), preferred_element_type=F32)
            for d in range(3):
                at = (pair * 9 + 3 * j + d) * C
                piece = part[:, d * C:(d + 1) * C]
                if fresh:
                    acc[at:at + C, :] = piece
                else:
                    acc[at:at + C, :] += piece

    def own(q):
        return acc[q * R:(q + 1) * R, :]

    def send_sums(blocks):
        for q in blocks:
            @pl.when(me_p != q)
            def _():
                sr[q] = own(q).astype(BF16)
                to_owner(q).start()

    for t in range(T):
        for r in range(2):
            final = t == T - 1

            def arrived(name):
                if r == 0:
                    local[name].wait()

            if t == 0:
                arrived("g")
            else:
                @pl.when(last)
                def _():
                    losses[t, r].wait()

                @pl.when(jnp.logical_not(last))
                def _():
                    steps[t - 1, r].wait_recv()
            if r == 1:
                for name in groups[t]:
                    moved[name].wait_recv()
                send_group(t + 2)
            ga, gb = 2 * r, 2 * r + 1
            grad = gs[t, r].astype(F32)
            spread(ga, grad)
            if t == 0 and r == 0:
                for c in weights[1]:
                    c.wait()
            arrived(("h", t))
            hidden = hs[t, r]
            fresh = t == 0 and r == 0
            if final:
                weight_grad(ga, 1, hidden, fresh)
                if r == 1:
                    send_sums(range(N // 2, N))
            grad_h = jnp.where(hidden.astype(F32) > 0, conv(ga, 1), 0.0)
            spread(gb, grad_h)
            if t == 0 and r == 0:
                for c in weights[0]:
                    c.wait()
            arrived(("x", t))
            inputs = xs[t, r]
            if final:
                weight_grad(gb, 0, inputs, fresh)
                if r == 1:
                    send_sums(range(N // 2))
            grad_u = conv(gb, 0)
            ob[t, r] = (grad + jnp.where(inputs.astype(F32) > 0, grad_u, 0.0)).astype(BF16)
            if final:
                if r == 0:
                    edge_home.start()
                else:
                    edge_away.start()
            else:
                @pl.when(me_s > 0)
                def _():
                    steps[t, r].start()

                weight_grad(ga, 1, hidden, fresh)
                weight_grad(gb, 0, inputs, fresh)

    for q in range(N):
        @pl.when(me_p == q)
        def _():
            kg_ref[...] = own(q)
    for p in range(N):
        @pl.when(me_p != p)
        def _():
            from_shard(p).wait_recv()
            kg_ref[...] += rr[p].astype(F32)
    kg_ref[...] *= 1.0 / float(E * E)

    edge_home.wait()
    edge_away.wait()
    for c in moved.values():
        c.wait_send()

    @pl.when(me_s > 0)
    def _():
        for c in steps.values():
            c.wait_send()

    for q in range(N):
        @pl.when(me_p != q)
        def _():
            to_owner(q).wait_send()


def on_device(saved_x, saved_h, kernels, grad_in, loss_grads):
    S, N = lax.axis_size("section"), lax.axis_size("dp")
    T, E, C = saved_x.shape[1], saved_x.shape[4], saved_x.shape[6]
    M = E * E * saved_x.shape[3]
    R = 18 * C // N
    cfg = dict(S=S, N=N, T=T, E=E, C=C)
    DMA = pltpu.SemaphoreType.DMA
    kg, edge = pl.pallas_call(
        functools.partial(relay, cfg),
        out_shape=(jax.ShapeDtypeStruct((R, C), F32), jax.ShapeDtypeStruct((2, M, C), BF16)),
        in_specs=[pl.BlockSpec(memory_space=pltpu.HBM)] * 5,
        out_specs=(pl.BlockSpec(memory_space=pltpu.VMEM), pl.BlockSpec(memory_space=pltpu.HBM)),
        scratch_shapes=[
            pltpu.VMEM((T, 2, M, C), BF16),
            pltpu.VMEM((T, 2, M, C), BF16),
            pltpu.VMEM((T, 2, M, C), BF16),
            pltpu.VMEM((T, 2, M, C), BF16),
            pltpu.VMEM((2, C, 9 * C), BF16),
            pltpu.VMEM((4, M + 2 * E, 3 * C), BF16),
            pltpu.VMEM((18 * C, C), F32),
            pltpu.VMEM((N, R, C), BF16),
            pltpu.VMEM((N, R, C), BF16),
            DMA((2 * T + 1,)),
            DMA((2, 9)),
            DMA((T, 2)),
            DMA((2 * T + 1,)),
            DMA((2 * T + 1,)),
            DMA((T, 2)),
            DMA((T, 2)),
            DMA((1,)),
            DMA((1,)),
            DMA((1,)),
            DMA((N,)),
            DMA((N,)),
        ],
        compiler_params=pltpu.CompilerParams(
            collective_id=0, has_side_effects=True, vmem_limit_bytes=63 * 1024 * 1024),
        cost_estimate=pl.CostEstimate(
            flops=48 * T * M * 9 * C * C // 6, bytes_accessed=3_000_000, transcendentals=0),
        name="relay",
    )(
        saved_x.reshape(2, T, M, C),
        saved_h.reshape(2, T, M, C),
        kernels.reshape(2, 2, 9, C, C),
        grad_in.reshape(2, M, C),
        loss_grads.reshape(2, T - 1, M, C),
    )
    return kg[None], edge.reshape(2, 1, 1, E, E, C)


def solution(mesh):
    return jax.shard_map(
        on_device,
        mesh=mesh,
        in_specs=(
            P(None, None, "section", "dp", None, None, None),
            P(None, None, "section", "dp", None, None, None),
            P("section", None, None, None, None, None),
            P(None, "section", "dp", None, None, None),
            P(None, None, "dp", None, None, None),
        ),
        out_specs=(P("section", "dp", None), P(None, "section", "dp", None, None, None)),
        check_vma=False,
    )
```

```python
import functools

import jax
import jax.numpy as jnp
from jax import lax
from jax.experimental import pallas as pl
from jax.experimental.pallas import tpu as pltpu
from jax.sharding import PartitionSpec as P

MESH = pl.DeviceIdType.MESH
F32 = jnp.float32
BF16 = jnp.bfloat16


def dims(cfg):
    return cfg["S"], cfg["N"], cfg["T"], cfg["E"], cfg["C"]


def relay(cfg, x_hbm, h_hbm, w_hbm, g_hbm, l_hbm, kg_ref, edge_hbm,
          xs, hs, gs, ob, wc, vb, acc, rr, sr,
          in_sem, w_sem, l_sem, ms, mr, ts, tr, es, er, lsem, rs_s, rs_r):
    S, N, T, E, C = dims(cfg)
    M = E * E
    R = 18 * C // N
    me_s = lax.axis_index("section")
    me_p = lax.axis_index("dp")
    mirror = S - 1 - me_s
    first = me_s == 0
    last = me_s == S - 1

    local = {}
    local["g"] = pltpu.make_async_copy(g_hbm.at[0], gs.at[0, 0], in_sem.at[0])
    for t in range(T):
        local["h", t] = pltpu.make_async_copy(h_hbm.at[0, t], hs.at[t, 0], in_sem.at[1 + 2 * t])
        local["x", t] = pltpu.make_async_copy(x_hbm.at[0, t], xs.at[t, 0], in_sem.at[2 + 2 * t])
    weights = []
    for pair in range(2):
        weights.append([
            pltpu.make_async_copy(
                w_hbm.at[0, pair, k], wc.at[pair, :, pl.ds(k * C, C)], w_sem.at[pair, k])
            for k in range(9)
        ])
    losses = {
        (t, r): pltpu.make_async_copy(l_hbm.at[r, t - 1], gs.at[t, r], l_sem.at[t - 1, r])
        for t in range(1, T) for r in range(2)
    }
    local["g"].start()
    for c in weights[1]:
        c.start()
    local["h", 0].start()
    for c in weights[0]:
        c.start()
    local["x", 0].start()
    for t in range(1, T):
        local["h", t].start()
        local["x", t].start()

    @pl.when(last)
    def _():
        for c in losses.values():
            c.start()

    barrier = pltpu.get_barrier_semaphore()
    pl.semaphore_signal(barrier, inc=1, device_id=(mirror, me_p), device_id_type=MESH)

    @pl.when(me_s > 0)
    def _():
        pl.semaphore_signal(barrier, inc=1, device_id=(me_s - 1, me_p), device_id_type=MESH)

    @pl.when(me_s < S - 1)
    def _():
        pl.semaphore_signal(barrier, inc=1, device_id=(me_s + 1, me_p), device_id_type=MESH)

    for q in range(N):
        @pl.when(me_p != q)
        def _():
            pl.semaphore_signal(barrier, inc=1, device_id=(me_s, q), device_id_type=MESH)

    greeted = N + (me_s > 0).astype(jnp.int32) + (me_s < S - 1).astype(jnp.int32)
    pl.semaphore_wait(barrier, greeted)

    def to_mirror(src, dst, i):
        return pltpu.make_async_remote_copy(
            src_ref=src, dst_ref=dst, send_sem=ms.at[i], recv_sem=mr.at[i],
            device_id=(mirror, me_p), device_id_type=MESH)

    moved = {"g": to_mirror(g_hbm.at[1], gs.at[0, 1], 0)}
    for t in range(T):
        moved["h", t] = to_mirror(h_hbm.at[1, t], hs.at[t, 1], 1 + 2 * t)
        moved["x", t] = to_mirror(x_hbm.at[1, t], xs.at[t, 1], 2 + 2 * t)
    groups = [["g", ("h", 0), ("x", 0)]] + [[("h", t), ("x", t)] for t in range(1, T)]

    def send_group(t):
        if t < T:
            for name in groups[t]:
                moved[name].start()

    send_group(0)
    send_group(1)

    steps = {
        (t, r): pltpu.make_async_remote_copy(
            src_ref=ob.at[t, r], dst_ref=gs.at[t + 1, r], send_sem=ts.at[t, r],
            recv_sem=tr.at[t, r], device_id=(me_s - 1, me_p), device_id_type=MESH)
        for t in range(T - 1) for r in range(2)
    }
    edge_home = pltpu.make_async_copy(ob.at[T - 1, 0], edge_hbm.at[0], lsem.at[0])
    edge_away = pltpu.make_async_remote_copy(
        src_ref=ob.at[T - 1, 1], dst_ref=edge_hbm.at[1], send_sem=es.at[0], recv_sem=er.at[0],
        device_id=(mirror, me_p), device_id_type=MESH)

    def to_owner(q):
        return pltpu.make_async_remote_copy(
            src_ref=sr.at[q], dst_ref=rr.at[me_p], send_sem=rs_s.at[q], recv_sem=rs_r.at[me_p],
            device_id=(me_s, q), device_id_type=MESH)

    def from_shard(p):
        return pltpu.make_async_remote_copy(
            src_ref=sr.at[p], dst_ref=rr.at[p], send_sem=rs_s.at[p], recv_sem=rs_r.at[p],
            device_id=(me_s, p), device_id_type=MESH)

    column = lax.broadcasted_iota(jnp.int32, (M, C), 0) % E
    low = column == 0
    high = column == E - 1
    for i in range(4):
        vb[i, 0:E, :] = jnp.zeros((E, 3 * C), BF16)
        vb[i, E + M:2 * E + M, :] = jnp.zeros((E, 3 * C), BF16)

    def spread(i, value):
        back = jnp.where(high, 0.0, pltpu.roll(value, M - 1, axis=0))
        ahead = jnp.where(low, 0.0, pltpu.roll(value, 1, axis=0))
        vb[i, E:E + M, 0:C] = back.astype(BF16)
        vb[i, E:E + M, C:2 * C] = value.astype(BF16)
        vb[i, E:E + M, 2 * C:3 * C] = ahead.astype(BF16)

    def rows(i, j):
        start = E - E * (j - 1)
        return vb[i, start:start + M, :]

    def conv(i, pair):
        total = None
        for j in range(3):
            part = lax.dot_general(
                rows(i, j), wc[pair, :, 3 * C * j:3 * C * (j + 1)],
                (((1,), (1,)), ((), ())), preferred_element_type=F32)
            total = part if total is None else total + part
        return total

    def weight_grad(i, pair, act, fresh):
        turned = jnp.maximum(act, 0).T
        for j in range(3):
            part = jnp.dot(turned, rows(i, j), preferred_element_type=F32)
            for d in range(3):
                at = (pair * 9 + 3 * j + d) * C
                piece = part[:, d * C:(d + 1) * C]
                if fresh:
                    acc[at:at + C, :] = piece
                else:
                    acc[at:at + C, :] += piece

    def own(q):
        return acc[q * R:(q + 1) * R, :]

    def send_sums(blocks):
        for q in blocks:
            @pl.when(me_p != q)
            def _():
                sr[q] = own(q).astype(BF16)
                to_owner(q).start()

    for n in range(T + 1):
        for t, r in [c for c in ((n, 0), (n - 1, 1)) if 0 <= c[0] < T]:
            final = t == T - 1

            def arrived(name):
                if r == 0:
                    local[name].wait()

            if t == 0:
                arrived("g")
            else:
                @pl.when(last)
                def _():
                    losses[t, r].wait()

                @pl.when(jnp.logical_not(last))
                def _():
                    steps[t - 1, r].wait_recv()
            if r == 1:
                for name in groups[t]:
                    moved[name].wait_recv()
                send_group(t + 2)
            ga, gb = 2 * r, 2 * r + 1
            grad = gs[t, r].astype(F32)
            spread(ga, grad)
            if t == 0 and r == 0:
                for c in weights[1]:
                    c.wait()
            arrived(("h", t))
            hidden = hs[t, r]
            fresh = t == 0 and r == 0
            if final:
                weight_grad(ga, 1, hidden, fresh)
                if r == 1:
                    send_sums(range(N // 2, N))
            grad_h = jnp.where(hidden.astype(F32) > 0, conv(ga, 1), 0.0)
            spread(gb, grad_h)
            if t == 0 and r == 0:
                for c in weights[0]:
                    c.wait()
            arrived(("x", t))
            inputs = xs[t, r]
            if final:
                weight_grad(gb, 0, inputs, fresh)
                if r == 1:
                    send_sums(range(N // 2))
            grad_u = conv(gb, 0)
            ob[t, r] = (grad + jnp.where(inputs.astype(F32) > 0, grad_u, 0.0)).astype(BF16)
            if final:
                if r == 0:
                    edge_home.start()
                else:
                    edge_away.start()
            else:
                @pl.when(me_s > 0)
                def _():
                    steps[t, r].start()

                weight_grad(ga, 1, hidden, fresh)
                weight_grad(gb, 0, inputs, fresh)

    total = acc[pl.ds(pl.multiple_of(me_p * R, R), R), :]
    for k in range(1, N):
        p = lax.rem(me_p + k, N)
        from_shard(p).wait_recv()
        total = total + rr[p].astype(F32)
    kg_ref[...] = total * (1.0 / float(E * E))

    edge_home.wait()
    edge_away.wait()
    for c in moved.values():
        c.wait_send()

    @pl.when(me_s > 0)
    def _():
        for c in steps.values():
            c.wait_send()

    for q in range(N):
        @pl.when(me_p != q)
        def _():
            to_owner(q).wait_send()


def on_device(saved_x, saved_h, kernels, grad_in, loss_grads):
    S, N = lax.axis_size("section"), lax.axis_size("dp")
    T, E, C = saved_x.shape[1], saved_x.shape[4], saved_x.shape[6]
    M = E * E * saved_x.shape[3]
    R = 18 * C // N
    cfg = dict(S=S, N=N, T=T, E=E, C=C)
    DMA = pltpu.SemaphoreType.DMA
    kg, edge = pl.pallas_call(
        functools.partial(relay, cfg),
        out_shape=(jax.ShapeDtypeStruct((R, C), F32), jax.ShapeDtypeStruct((2, M, C), BF16)),
        in_specs=[pl.BlockSpec(memory_space=pltpu.HBM)] * 5,
        out_specs=(pl.BlockSpec(memory_space=pltpu.VMEM), pl.BlockSpec(memory_space=pltpu.HBM)),
        scratch_shapes=[
            pltpu.VMEM((T, 2, M, C), BF16),
            pltpu.VMEM((T, 2, M, C), BF16),
            pltpu.VMEM((T, 2, M, C), BF16),
            pltpu.VMEM((T, 2, M, C), BF16),
            pltpu.VMEM((2, C, 9 * C), BF16),
            pltpu.VMEM((4, M + 2 * E, 3 * C), BF16),
            pltpu.VMEM((18 * C, C), F32),
            pltpu.VMEM((N, R, C), BF16),
            pltpu.VMEM((N, R, C), BF16),
            DMA((2 * T + 1,)),
            DMA((2, 9)),
            DMA((T, 2)),
            DMA((2 * T + 1,)),
            DMA((2 * T + 1,)),
            DMA((T, 2)),
            DMA((T, 2)),
            DMA((1,)),
            DMA((1,)),
            DMA((1,)),
            DMA((N,)),
            DMA((N,)),
        ],
        compiler_params=pltpu.CompilerParams(
            collective_id=0, has_side_effects=True, vmem_limit_bytes=63 * 1024 * 1024),
        cost_estimate=pl.CostEstimate(
            flops=48 * T * M * 9 * C * C // 6, bytes_accessed=3_000_000, transcendentals=0),
        name="relay",
    )(
        saved_x.reshape(2, T, M, C),
        saved_h.reshape(2, T, M, C),
        kernels.reshape(2, 2, 9, C, C),
        grad_in.reshape(2, M, C),
        loss_grads.reshape(2, T - 1, M, C),
    )
    return kg[None], edge.reshape(2, 1, 1, E, E, C)


def solution(mesh):
    return jax.shard_map(
        on_device,
        mesh=mesh,
        in_specs=(
            P(None, None, "section", "dp", None, None, None),
            P(None, None, "section", "dp", None, None, None),
            P("section", None, None, None, None, None),
            P(None, "section", "dp", None, None, None),
            P(None, None, "dp", None, None, None),
        ),
        out_specs=(P("section", "dp", None), P(None, "section", "dp", None, None, None)),
        check_vma=False,
    )
```
